32 devices in a mesh: dp: 16 (over z, x, core), tensor: 2 (over y).
Axes of the slice: x: 2, y: 2, z: 4, core: 2. Of those that a mesh axis runs over, the one named last changes fastest.
Arguments:
- hidden_in: bfloat16 [16384, 1024], P(('dp', 'tensor')), may hold values from -6 to 6
- seq_lengths: int32 [16, 8], P('dp'), may hold values from 0 to 1024, as said below
- attn_gain: float32 [1024], replicated, may hold values from 0.5 to 1.5
- w_query: bfloat16 [1024, 2048], P(None, 'tensor'), may hold values from -0.1875 to 0.1875
- key_weight: bfloat16 [1024, 1024], P(None, 'tensor'), may hold values from -0.1875 to 0.1875
- value_weight: bfloat16 [1024, 1024], P(None, 'tensor'), may hold values from -0.1875 to 0.1875
- q_gain: float32 [128], replicated, may hold values from 0.25 to 1.75
- k_gain: float32 [128], replicated, may hold values from 0.25 to 1.75
- w_out: bfloat16 [2048, 1024], P('tensor'), may hold values from -0.75 to 0.75
- ffn_gain: float32 [1024], replicated, may hold values from 0.5 to 1.5
- w_gate: bfloat16 [1024, 3072], P(None, 'tensor'), may hold values from -0.1875 to 0.1875
- w_up: bfloat16 [1024, 3072], P(None, 'tensor'), may hold values from -0.1875 to 0.1875
- w_down: bfloat16 [3072, 1024], P('tensor'), may hold values from -0.21875 to 0.21875
- out_grad: bfloat16 [16384, 1024], P(('dp', 'tensor')), may hold values from -6 to 6
Outputs:
- mixed: bfloat16 [16384, 1024], P(('dp', 'tensor'))
- input_grad: float32 [16384, 1024], P(('dp', 'tensor'))
- grad_attn_gain: float32 [1024], replicated
- grad_query: float32 [1024, 2048], P('dp', 'tensor')
- grad_key: float32 [1024, 1024], P('dp', 'tensor')
- grad_value: float32 [1024, 1024], P('dp', 'tensor')
- grad_q_gain: float32 [128], replicated
- grad_k_gain: float32 [128], replicated
- grad_out: float32 [2048, 1024], P('tensor', 'dp')
- grad_ffn_gain: float32 [1024], replicated
- grad_gate: float32 [1024, 3072], P('dp', 'tensor')
- grad_up: float32 [1024, 3072], P('dp', 'tensor')
- grad_down: float32 [3072, 1024], P('tensor', 'dp')
The draws below stay inside these ranges and needn't reach their ends.
Inputs may be any that keep to these rules, and one draw needn't show every extreme that they name: `seq_lengths`: row i lists the lengths of the sequences packed on index i of dp in packing order: nonzero lengths first, each from 128 to 1024, then zeros. A row sums to 1024 at most; some row holds only sequences of exactly 1024 and fills all 1024 positions.
All inputs are finite; a program needn't handle non-finite values.
Results may differ from the reference program's by a relative error of at most 0.015.
Values may be sent and summed in bfloat16 or wider, within the bound.
A program may use at most 192 MiB of HBM per device.

```python
import math
import jax
import jax.numpy as jnp
from jax import lax

MODEL_WIDTH = 1024
QUERY_HEADS = 16
KEY_VALUE_HEADS = 8
HEAD_WIDTH = 128
FF = 3072
TOKENS_PER_SHARD = 1024
MIN_LEN = 128
SEQ_MAX = 1024
SLOTS = 8
TOKENS = 16384
N_DP = 16


def draw_seq_lengths(key, part):
    key_len, key_target, key_heavy = jax.random.split(key, 3)
    lengths = jax.random.randint(key_len, (N_DP, SLOTS), MIN_LEN, SEQ_MAX + 1)
    targets = jax.random.randint(key_target, (N_DP, 1), TOKENS_PER_SHARD // 2, TOKENS_PER_SHARD + 1)
    row_ends = jnp.cumsum(lengths, axis=1)
    keeping = row_ends <= targets
    kept_sum = jnp.sum(jnp.where(keeping, lengths, 0), axis=1, keepdims=True)
    kept_count = jnp.sum(keeping.astype(jnp.int32), axis=1, keepdims=True)
    remain = targets - kept_sum
    slot_index = jnp.arange(SLOTS)[None, :]
    filler = jnp.where((slot_index == kept_count) & (remain >= MIN_LEN), jnp.minimum(remain, SEQ_MAX), 0)
    lengths = jnp.where(keeping, lengths, filler)
    heavy_row = jax.random.randint(key_heavy, (), 0, N_DP)
    full_row = jnp.where(slot_index < TOKENS_PER_SHARD // SEQ_MAX, SEQ_MAX, 0)
    lengths = jnp.where(jnp.arange(N_DP)[:, None] == heavy_row, full_row, lengths)
    return lengths.astype(jnp.int32)


def strengthened(values, stream_key, source, target, shards_of, factor):
    owner, partner = [(jnp.arange(values.shape[dim]) // (values.shape[dim] // shards_of)).reshape([-1 if axis == dim else 1 for axis in range(values.ndim)]) for dim in (source, target)]
    chosen = jax.random.permutation(stream_key, shards_of)[partner]
    strong = (owner == chosen) | (owner == (partner + shards_of // 2) % shards_of)
    return jnp.where(strong, factor * values, values)


def shard_levels(own_key, dims, cuts, least, top_value):
    def one(dim, shards_of):
        steps = jax.random.uniform(jax.random.fold_in(jax.random.fold_in(own_key, 6), dim), (shards_of,), jnp.float32, least / len(cuts), top_value / len(cuts))
        return jnp.repeat(jnp.exp(steps), dims[dim] // shards_of).reshape((-1,) + (1,) * (len(dims) - dim - 1))

    gain = one(*cuts[0])
    for cut in cuts[1:]:
        gain = gain * one(*cut)
    return gain


def gaussian(rng, dims, deviation, bound, shards=(), kind=jnp.bfloat16):
    drawn = jax.random.normal(rng, dims, jnp.float32) * deviation
    if len(shards) > 0:
        drawn = shard_levels(rng, dims, shards, -0.22, 0.18) * drawn
    return jnp.clip(drawn, min=-bound, max=bound).astype(kind)


def gaussian_with(rng, extent, width, limit, shards, heavy, held_as=jnp.bfloat16):
    entries = width * jax.random.normal(rng, extent, jnp.float32)
    if shards:
        entries = entries * shard_levels(rng, extent, shards, -0.22, 0.18)
    return jnp.clip(strengthened(entries, jax.random.fold_in(rng, 3), *heavy), -limit, limit).astype(held_as)


def setup_inputs(seed: int = 0) -> dict:
    arg_keys = jax.random.split(jax.random.key(seed), 15)
    return {
        "hidden_in": gaussian(arg_keys[0], (TOKENS, MODEL_WIDTH), 1.0, 6.0, ((0, 32),)),
        "seq_lengths": draw_seq_lengths(jax.random.fold_in(arg_keys[14], 71), 0),
        "attn_gain": jnp.clip(1.0 + 0.1 * jax.random.normal(arg_keys[2], (MODEL_WIDTH,), jnp.float32), 0.5, 1.5),
        "w_query": gaussian(arg_keys[3], (MODEL_WIDTH, QUERY_HEADS * HEAD_WIDTH), MODEL_WIDTH ** -0.5, 0.1875, ((1, 2),)),
        "key_weight": gaussian(arg_keys[4], (MODEL_WIDTH, KEY_VALUE_HEADS * HEAD_WIDTH), MODEL_WIDTH ** -0.5, 0.1875, ((1, 2),)),
        "value_weight": gaussian(arg_keys[5], (MODEL_WIDTH, KEY_VALUE_HEADS * HEAD_WIDTH), MODEL_WIDTH ** -0.5, 0.1875, ((1, 2),)),
        "q_gain": jnp.clip(1.0 + 0.15 * jax.random.normal(arg_keys[6], (HEAD_WIDTH,), jnp.float32), 0.25, 1.75),
        "k_gain": jnp.clip(1.0 + 0.15 * jax.random.normal(arg_keys[7], (HEAD_WIDTH,), jnp.float32), 0.25, 1.75),
        "w_out": gaussian(arg_keys[8], (QUERY_HEADS * HEAD_WIDTH, MODEL_WIDTH), (QUERY_HEADS * HEAD_WIDTH // 32) ** -0.5, 0.75, ((0, 2),)),
        "ffn_gain": jnp.clip(1.0 + 0.1 * jax.random.normal(arg_keys[9], (MODEL_WIDTH,), jnp.float32), 0.5, 1.5),
        "w_gate": gaussian(arg_keys[10], (MODEL_WIDTH, FF), MODEL_WIDTH ** -0.5, 0.1875, ((1, 2),)),
        "w_up": gaussian(arg_keys[11], (MODEL_WIDTH, FF), MODEL_WIDTH ** -0.5, 0.1875, ((1, 2),)),
        "w_down": gaussian(arg_keys[12], (FF, MODEL_WIDTH), (FF // 4) ** -0.5, 0.21875, ((0, 2),)),
        "out_grad": gaussian_with(arg_keys[13], (TOKENS, MODEL_WIDTH), 1.0, 6.0, ((0, 32),), (0, 1, 32, 2.75)),
    }


EPSILON = 1e-06
ROPE_BASE = 1000000.0
MASK_FILL = -1e+30
PRECISE = lax.Precision.HIGHEST

@jax.custom_vjp
def lower_bound(v):
    return lax.optimization_barrier(v.astype(jnp.bfloat16)).astype(jnp.float32)

@jax.custom_vjp
def lower_bound_backward(v):
    return v

def low_keep(v):
    return (lower_bound(v), None)

def low_pass(kept, grad):
    return (grad,)

def back_keep(v):
    return (v, None)

def back_low(kept, grad):
    return (lower_bound(grad),)
lower_bound.defvjp(low_keep, low_pass)
lower_bound_backward.defvjp(back_keep, back_low)

def matrix_product(left, right):
    return jnp.dot(left, right, precision=PRECISE, preferred_element_type=jnp.float32)

def rms_scale(vectors):
    return lax.rsqrt(lax.optimization_barrier(jnp.mean(vectors * vectors, axis=-1, keepdims=True)) + EPSILON)

def layout(lengths):
    row_ends = jnp.cumsum(lengths).astype(jnp.int32)
    block_locations = jnp.arange(TOKENS_PER_SHARD, dtype=jnp.int32)
    before = row_ends[None, :] <= block_locations[:, None]
    sequence_label = lax.optimization_barrier(jnp.sum(before.astype(jnp.int32), axis=1)).astype(jnp.int32)
    starts = lax.optimization_barrier(jnp.sum(jnp.where(before, lengths[None, :], 0), axis=1)).astype(jnp.int32)
    return (sequence_label, block_locations - starts)

def rotary(position):
    half_size = HEAD_WIDTH // 2
    frequency = jnp.power(ROPE_BASE, -(jnp.arange(half_size, dtype=jnp.float32) * 2.0 / HEAD_WIDTH))
    angles = position.astype(jnp.float32)[:, None] * frequency[None, :]
    angles = jnp.concatenate([angles, angles], axis=1)
    return (jnp.cos(angles)[:, None, :], jnp.sin(angles)[:, None, :])

def rotate(vectors):
    half_size = vectors.shape[-1] // 2
    return jnp.concatenate([-vectors[..., half_size:], vectors[..., :half_size]], axis=-1)

def head_map(vectors, gain_vec, cosine, sine):
    normalized = vectors * rms_scale(vectors) * gain_vec
    return normalized * cosine + rotate(normalized) * sine

def attend(query_rotated, key_rot, value_rows, sequence_label):
    group_width = QUERY_HEADS // KEY_VALUE_HEADS
    rows_per_block = min(512, TOKENS_PER_SHARD)
    block_count = TOKENS_PER_SHARD // rows_per_block
    block_locations = jnp.arange(TOKENS_PER_SHARD, dtype=jnp.int32)

    def single_block(inputs):
        qblock, q_segment, q_places = inputs
        scores = lower_bound_backward(jnp.einsum('qkgd,tkd->qkgt', qblock, key_rot, precision=PRECISE) * (1.0 / math.sqrt(HEAD_WIDTH)))
        allowed = (q_segment[:, None] == sequence_label[None, :]) & (q_places[:, None] >= block_locations[None, :]) & (q_segment[:, None] < SLOTS)
        allowed_mask = allowed[:, None, None, :]
        row_max = lax.optimization_barrier(jnp.max(jnp.where(allowed_mask, scores, MASK_FILL), axis=-1, keepdims=True))
        exp_terms = jnp.exp(jnp.where(allowed_mask, scores - row_max, MASK_FILL))
        row_sum = lax.optimization_barrier(jnp.sum(exp_terms, axis=-1, keepdims=True))
        soft_weights = lower_bound(exp_terms / jnp.where(row_sum > 0.0, row_sum, 1.0))
        return jnp.einsum('qkgt,tkd->qkgd', soft_weights, value_rows, precision=PRECISE)
    final_output = lax.map(jax.checkpoint(single_block), (query_rotated.reshape(block_count, rows_per_block, KEY_VALUE_HEADS, group_width, HEAD_WIDTH), sequence_label.reshape(block_count, rows_per_block), block_locations.reshape(block_count, rows_per_block)))
    return final_output.reshape(TOKENS_PER_SHARD, QUERY_HEADS * HEAD_WIDTH)

def layer(resid_in, lengths, params):
    attn_gain, w_query, key_weight, value_weight, q_gain, k_gain, w_out, ffn_gain, w_gate, w_up, w_down = params
    sequence_label, position = layout(lengths)
    cosine, sine = rotary(position)
    normalized = lower_bound(resid_in * rms_scale(resid_in) * attn_gain)
    q_raw = lower_bound_backward(matrix_product(normalized, w_query)).reshape(TOKENS_PER_SHARD, QUERY_HEADS, HEAD_WIDTH)
    key_unrotated = lower_bound_backward(matrix_product(normalized, key_weight)).reshape(TOKENS_PER_SHARD, KEY_VALUE_HEADS, HEAD_WIDTH)
    value_rows = lower_bound(lower_bound_backward(matrix_product(normalized, value_weight))).reshape(TOKENS_PER_SHARD, KEY_VALUE_HEADS, HEAD_WIDTH)
    query_rotated = lower_bound(head_map(q_raw, q_gain, cosine, sine))
    key_rot = lower_bound(head_map(key_unrotated, k_gain, cosine, sine))
    attn_out = lower_bound(lower_bound_backward(attend(query_rotated, key_rot, value_rows, sequence_label)))
    resid_mid = resid_in + lower_bound_backward(matrix_product(attn_out, w_out))
    mid = lower_bound(resid_mid * rms_scale(resid_mid) * ffn_gain)
    gate_pre = lower_bound_backward(matrix_product(mid, w_gate))
    up_pre = lower_bound_backward(matrix_product(mid, w_up))
    hidden = lower_bound(jax.nn.silu(gate_pre) * up_pre)
    return resid_mid + lower_bound_backward(matrix_product(hidden, w_down))

def reference(hidden_in, seq_lengths, attn_gain, w_query, key_weight, value_weight, q_gain, k_gain, w_out, ffn_gain, w_gate, w_up, w_down, out_grad):
    params = tuple((item.astype(jnp.float32) for item in (attn_gain, w_query, key_weight, value_weight, q_gain, k_gain, w_out, ffn_gain, w_gate, w_up, w_down)))
    resid_in = hidden_in.astype(jnp.float32).reshape(N_DP, TOKENS_PER_SHARD, MODEL_WIDTH)

    def forward(resid_all, weights):

        def scan_step(carry, inputs):
            return (carry, jax.checkpoint(layer)(inputs[0], inputs[1], weights))
        return lax.scan(scan_step, None, (resid_all, seq_lengths))[1]
    mixed, pullback = jax.vjp(forward, resid_in, params)
    grad_input, grad_weights = pullback(out_grad.astype(jnp.float32).reshape(N_DP, TOKENS_PER_SHARD, MODEL_WIDTH))
    return (mixed.reshape(TOKENS, MODEL_WIDTH).astype(jnp.bfloat16), grad_input.reshape(TOKENS, MODEL_WIDTH), grad_weights[0], grad_weights[1], grad_weights[2], grad_weights[3], grad_weights[4], grad_weights[5], grad_weights[6], grad_weights[7], grad_weights[8], grad_weights[9], grad_weights[10])
```

```python
import math

import jax
import jax.numpy as jnp
from jax import lax
from jax.experimental import pallas as pl
from jax.experimental.pallas import tpu as pltpu
from jax.sharding import PartitionSpec as P

EPSILON = 1e-06
ROPE_BASE = 1000000.0
MASK_FILL = -1e30
BF16 = jnp.bfloat16
F32 = jnp.float32
VMEM_LIMIT = 56 * 1024 * 1024


def rms_scale(vectors):
    return lax.rsqrt(jnp.mean(vectors * vectors, axis=-1, keepdims=True) + EPSILON)


def dot_nn(left, right):
    return jnp.dot(left, right, preferred_element_type=F32)


def dot_tn(left, right):
    return lax.dot_general(left, right, (((0,), (0,)), ((), ())), preferred_element_type=F32)


def dot_nt(left, right):
    return lax.dot_general(left, right, (((1,), (1,)), ((), ())), preferred_element_type=F32)


def swap(array):
    return lax.ppermute(array, "tensor", [(0, 1), (1, 0)])


def layout(lengths, tokens):
    slots = jnp.arange(lengths.shape[0], dtype=jnp.int32)
    row_ends = jnp.sum(jnp.where(slots[None, :] <= slots[:, None], lengths[None, :], 0), axis=1)
    places = jnp.arange(tokens, dtype=jnp.int32)
    before = row_ends[None, :] <= places[:, None]
    label = jnp.sum(before.astype(jnp.int32), axis=1)
    starts = jnp.sum(jnp.where(before, lengths[None, :], 0), axis=1)
    first_key = jnp.where(label < lengths.shape[0], starts, tokens)
    return first_key, places - starts


def rotary(position, head_size):
    half = head_size // 2
    lane = jnp.arange(head_size, dtype=jnp.int32)
    frequency = jnp.power(ROPE_BASE, -((lane % half).astype(F32) * 2.0 / head_size))
    angles = position.astype(F32)[:, None] * frequency[None, :]
    sign = jnp.where(lane < half, -1.0, 1.0)
    return jnp.cos(angles), jnp.sin(angles) * sign[None, :]


def turn(raw, gain, cosine, sine):
    normalized = raw * rms_scale(raw) * gain
    half = raw.shape[-1] // 2
    return (normalized * cosine + pltpu.roll(normalized, half, 1) * sine).astype(BF16)


def turn_back(raw, gain, cosine, sine, grad):
    half = raw.shape[-1] // 2
    scale = rms_scale(raw)
    unit = raw * scale
    turned = grad * cosine - pltpu.roll(grad, half, 1) * sine
    gain_grad = jnp.sum(turned * unit, axis=0, keepdims=True)
    weighted = turned * gain
    back = scale * (weighted - unit * jnp.mean(weighted * unit, axis=-1, keepdims=True))
    return back.astype(BF16), gain_grad


def halves(share, me):
    own = pl.ds(pl.multiple_of(me * share, share), share)
    other = pl.ds(pl.multiple_of((1 - me) * share, share), share)
    return own, other


def forward_kernel(
    block, me_ref, q_own, q_oth, k_own, k_oth, v_own, v_oth, cos_ref, sin_ref, qg, kg, first_ref,
    o_own, o_oth, lse_ref, q_rot, k_rot, v_all, out,
):
    share = q_own.shape[0]
    tokens, width = 2 * share, q_own.shape[1]
    factor = math.log2(math.e) / math.sqrt(width)
    rows = halves(share, me_ref[0])

    @pl.when(pl.program_id(1) == 0)
    def _():
        for place, k_ref, v_ref in zip(rows, (k_own, k_oth), (v_own, v_oth)):
            k_rot[place, :] = turn(k_ref[...], kg[...], cos_ref[place, :], sin_ref[place, :])
            v_all[place, :] = v_ref[...]

    for place, q_ref in zip(rows, (q_own, q_oth)):
        q_rot[place, :] = turn(q_ref[...], qg[...], cos_ref[place, :], sin_ref[place, :])
    for start in range(0, tokens, block):
        stop = start + block
        scores = dot_nt(q_rot[start:stop, :], k_rot[:stop, :])
        key = lax.broadcasted_iota(jnp.int32, scores.shape, 1)
        row = lax.broadcasted_iota(jnp.int32, scores.shape, 0) + start
        allowed = (key >= first_ref[start:stop, :]) & (key <= row)
        terms = jnp.exp2(jnp.where(allowed, scores * factor, MASK_FILL))
        total = jnp.sum(terms, axis=-1, keepdims=True)
        total = jnp.where(total > 0.0, total, 1.0)
        result = dot_nn(terms.astype(BF16), v_all[:stop, :]) / total
        out[start:stop, :] = result.astype(BF16)
        log_total = jnp.broadcast_to(jnp.log2(total), (block, width)).T
        lse_ref[0, :, start:stop] = log_total[0:1, :]
    o_own[...] = out[rows[0], :]
    o_oth[...] = out[rows[1], :]


def backward_kernel(
    block, me_ref, q_own, q_oth, k_own, k_oth, v_own, v_oth, cos_ref, sin_ref, qg, kg, first_ref,
    o_own, o_oth, d_own, d_oth, lse_ref,
    dq_own, dq_oth, dk_own, dk_oth, dv_own, dv_oth, gq_ref, gk_ref,
    q_rot, k_rot, v_all, d_all, delta, dq_all, dk_all, dv_all,
):
    share = q_own.shape[0]
    tokens, width = 2 * share, q_own.shape[1]
    root = 1.0 / math.sqrt(width)
    factor = math.log2(math.e) * root
    rows = halves(share, me_ref[0])
    head, part = pl.program_id(0), pl.program_id(1)

    @pl.when((head == 0) & (part == 0))
    def _():
        gq_ref[...] = jnp.zeros_like(gq_ref)
        gk_ref[...] = jnp.zeros_like(gk_ref)

    @pl.when(part == 0)
    def _():
        for place, k_ref, v_ref in zip(rows, (k_own, k_oth), (v_own, v_oth)):
            k_rot[place, :] = turn(k_ref[...], kg[...], cos_ref[place, :], sin_ref[place, :])
            v_all[place, :] = v_ref[...]
        dk_all[...] = jnp.zeros_like(dk_all)
        dv_all[...] = jnp.zeros_like(dv_all)

    for place, q_ref, o_ref, d_ref in zip(
        rows, (q_own, q_oth), (o_own, o_oth), (d_own, d_oth)
    ):
        q_rot[place, :] = turn(q_ref[...], qg[...], cos_ref[place, :], sin_ref[place, :])
        d_all[place, :] = d_ref[...]
        product = o_ref[...].astype(F32) * d_ref[...].astype(F32)
        delta[:, place] = jnp.sum(product.T, axis=0, keepdims=True)
    for start in range(0, tokens, block):
        stop = start + block
        q_rows = q_rot[start:stop, :]
        d_rows = d_all[start:stop, :]
        scores = dot_nt(k_rot[:stop, :], q_rows)
        key = lax.broadcasted_iota(jnp.int32, scores.shape, 0)
        row = lax.broadcasted_iota(jnp.int32, scores.shape, 1) + start
        allowed = (key >= first_ref[:, start:stop]) & (key <= row)
        shifted = scores * factor - lse_ref[0, :, start:stop]
        probs = jnp.exp2(jnp.where(allowed, shifted, MASK_FILL))
        d_probs = dot_nt(v_all[:stop, :], d_rows)
        d_scores = (probs * (d_probs - delta[:, start:stop])).astype(BF16)
        dv_all[:stop, :] += dot_nn(probs.astype(BF16), d_rows)
        dk_all[:stop, :] += dot_nn(d_scores, q_rows)
        dq_all[start:stop, :] = dot_tn(d_scores, k_rot[:stop, :]) * root
    for place, q_ref, dq_ref in zip(rows, (q_own, q_oth), (dq_own, dq_oth)):
        back, gain_grad = turn_back(
            q_ref[...], qg[...], cos_ref[place, :], sin_ref[place, :], dq_all[place, :]
        )
        dq_ref[...] = back
        gq_ref[...] += gain_grad

    @pl.when(part == pl.num_programs(1) - 1)
    def _():
        for place, k_ref, dk_ref, dv_ref in zip(
            rows, (k_own, k_oth), (dk_own, dk_oth), (dv_own, dv_oth)
        ):
            back, gain_grad = turn_back(
                k_ref[...], kg[...], cos_ref[place, :], sin_ref[place, :], dk_all[place, :] * root
            )
            dk_ref[...] = back
            gk_ref[...] += gain_grad
            dv_ref[...] = dv_all[place, :].astype(BF16)


def attention_specs(share, width, group):
    tokens = 2 * share
    by_query = pl.BlockSpec((share, width), lambda g, j, me: (0, g * group + j))
    by_key = pl.BlockSpec((share, width), lambda g, j, me: (0, g))
    table = pl.BlockSpec((tokens, width), lambda g, j, me: (0, 0))
    gain = pl.BlockSpec((1, width), lambda g, j, me: (0, 0))
    sums = pl.BlockSpec((1, 1, tokens), lambda g, j, me: (g * group + j, 0, 0))
    return by_query, by_key, table, gain, sums


def attention_forward(me, q, k, v, tables, gains, first_key, kv_here, group, width):
    share = q[0].shape[0]
    tokens = 2 * share
    block = min(256, tokens)
    by_query, by_key, table, gain, sums = attention_specs(share, width, group)
    column = pl.BlockSpec((tokens, 1), lambda g, j, me: (0, 0))
    rows_out = jax.ShapeDtypeStruct((share, kv_here * group * width), BF16)

    def body(*refs):
        forward_kernel(block, *refs)

    return pl.pallas_call(
        body,
        grid_spec=pltpu.PrefetchScalarGridSpec(
            num_scalar_prefetch=1,
            grid=(kv_here, group),
            in_specs=[by_query] * 2 + [by_key] * 4 + [table] * 2 + [gain] * 2 + [column],
            out_specs=[by_query, by_query, sums],
            scratch_shapes=[pltpu.VMEM((tokens, width), BF16)] * 4,
        ),
        out_shape=[
            rows_out,
            rows_out,
            jax.ShapeDtypeStruct((kv_here * group, 1, tokens), F32),
        ],
        compiler_params=pltpu.CompilerParams(vmem_limit_bytes=VMEM_LIMIT),
        cost_estimate=pl.CostEstimate(
            flops=4 * kv_here * group * tokens * tokens * width,
            bytes_accessed=12 * tokens * kv_here * group * width,
            transcendentals=kv_here * group * tokens * tokens,
        ),
    )(me, *q, *k, *v, *tables, *gains, first_key[:, None])


def attention_backward(
    me, q, k, v, tables, gains, first_key, outs, d_outs, totals, kv_here, group, width
):
    share = q[0].shape[0]
    tokens = 2 * share
    block = min(256, tokens)
    by_query, by_key, table, gain, sums = attention_specs(share, width, group)
    line = pl.BlockSpec((1, tokens), lambda g, j, me: (0, 0))
    q_out = jax.ShapeDtypeStruct((share, kv_here * group * width), BF16)
    k_out = jax.ShapeDtypeStruct((share, kv_here * width), BF16)
    gain_out = jax.ShapeDtypeStruct((1, width), F32)

    def body(*refs):
        backward_kernel(block, *refs)

    return pl.pallas_call(
        body,
        grid_spec=pltpu.PrefetchScalarGridSpec(
            num_scalar_prefetch=1,
            grid=(kv_here, group),
            in_specs=[by_query] * 2
            + [by_key] * 4
            + [table] * 2
            + [gain] * 2
            + [line]
            + [by_query] * 4
            + [sums],
            out_specs=[by_query] * 2 + [by_key] * 4 + [gain] * 2,
            scratch_shapes=[pltpu.VMEM((tokens, width), BF16)] * 4
            + [pltpu.VMEM((1, tokens), F32)]
            + [pltpu.VMEM((tokens, width), F32)] * 3,
        ),
        out_shape=[q_out] * 2 + [k_out] * 4 + [gain_out] * 2,
        compiler_params=pltpu.CompilerParams(vmem_limit_bytes=VMEM_LIMIT),
        cost_estimate=pl.CostEstimate(
            flops=10 * kv_here * group * tokens * tokens * width,
            bytes_accessed=20 * tokens * kv_here * group * width,
            transcendentals=kv_here * group * tokens * tokens,
        ),
    )(me, *q, *k, *v, *tables, *gains, first_key[None, :], *outs, *d_outs, totals)


def scatter_rows(partial, order):
    count = lax.axis_size("dp")
    me = lax.axis_index("dp")
    bits = count.bit_length() - 1
    columns = partial.shape[1]
    left = list(range(bits))[::-1]
    held = partial.reshape((2,) * bits + (partial.shape[0] // count, columns))
    for bit in order:
        axis = left.index(bit)
        mine = (me >> bit) & 1
        kept = lax.dynamic_index_in_dim(held, mine, axis, keepdims=False)
        sent = lax.dynamic_index_in_dim(held, 1 - mine, axis, keepdims=False)
        pairs = [(i, i ^ (1 << bit)) for i in range(count)]
        shape = sent.shape
        sent = sent.reshape(-1, columns)
        got = lax.ppermute(sent, "dp", pairs).reshape(shape)
        total = kept.astype(F32) + got.astype(F32)
        left.remove(bit)
        held = total.astype(BF16) if left else total
    return held


def sum_all(values):
    count = lax.axis_size("dp")
    values = values + swap(values)
    bit = 1
    while bit < count:
        values = values + lax.ppermute(values, "dp", [(i, i ^ bit) for i in range(count)])
        bit *= 2
    return values


def shards(
    hidden_in,
    seq_lengths,
    attn_gain,
    w_query,
    key_weight,
    value_weight,
    q_gain,
    k_gain,
    w_out,
    ffn_gain,
    w_gate,
    w_up,
    w_down,
    out_grad,
):
    width = q_gain.shape[0]
    tokens = 2 * hidden_in.shape[0]
    heads_here = w_query.shape[1] // width
    kv_here = key_weight.shape[1] // width
    group = heads_here // kv_here
    bits = lax.axis_size("dp").bit_length() - 1
    near = [0] + list(range(1, bits))
    far = [0] + list(range(2, bits)) + ([1] if bits > 1 else [])
    me = lax.axis_index("tensor").astype(jnp.int32).reshape(1)
    first_key, position = layout(seq_lengths[0], tokens)
    tables = rotary(position, width)
    gains = (q_gain[None, :], k_gain[None, :])

    resid_in = hidden_in.astype(F32)
    scale_in = rms_scale(resid_in)
    unit_in = resid_in * scale_in
    normed = (unit_in * attn_gain).astype(BF16)
    normed = (normed, swap(normed))
    grads = (out_grad, swap(out_grad))
    q_raw = [dot_nn(rows, w_query) for rows in normed]
    k_raw = [dot_nn(rows, key_weight) for rows in normed]
    values = [dot_nn(rows, value_weight).astype(BF16) for rows in normed]
    attn_own, attn_oth, totals = attention_forward(
        me, q_raw, k_raw, values, tables, gains, first_key, kv_here, group, width
    )
    out_got = swap(dot_nn(attn_oth, w_out).astype(BF16))
    resid_mid = resid_in + (dot_nn(attn_own, w_out) + out_got.astype(F32))
    scale_mid = rms_scale(resid_mid)
    unit_mid = resid_mid * scale_mid
    mid = (unit_mid * ffn_gain).astype(BF16)
    mid = (mid, swap(mid))

    hidden, d_up, d_gate = [], [], []
    for rows, grad_rows in zip(mid, grads):
        gate_pre = dot_nn(rows, w_gate)
        up_pre = dot_nn(rows, w_up)
        sigmoid = jax.nn.sigmoid(gate_pre)
        activated = gate_pre * sigmoid
        hidden.append((activated * up_pre).astype(BF16))
        d_hidden = dot_nt(grad_rows, w_down)
        d_up.append((d_hidden * activated).astype(BF16))
        d_gate.append(
            (d_hidden * up_pre * sigmoid * (1.0 + gate_pre * (1.0 - sigmoid))).astype(BF16)
        )
    d_mid_got = swap((dot_nt(d_gate[1], w_gate) + dot_nt(d_up[1], w_up)).astype(BF16))
    d_mid = dot_nt(d_gate[0], w_gate) + dot_nt(d_up[0], w_up) + d_mid_got.astype(F32)
    down_got = swap(dot_nn(hidden[1], w_down).astype(BF16))
    mixed = (resid_mid + (dot_nn(hidden[0], w_down) + down_got.astype(F32))).astype(BF16)

    mid_all = jnp.concatenate(mid, axis=0)
    grads_all = jnp.concatenate(grads, axis=0)
    g_gate = scatter_rows(dot_tn(mid_all, jnp.concatenate(d_gate, axis=0)).astype(BF16), near)
    g_up = scatter_rows(dot_tn(mid_all, jnp.concatenate(d_up, axis=0)).astype(BF16), far)
    g_down = scatter_rows(dot_tn(grads_all, jnp.concatenate(hidden, axis=0)).astype(BF16), near)

    g_ffn = jnp.sum(d_mid * unit_mid, axis=0)
    weighted_mid = d_mid * ffn_gain
    d_resid = out_grad.astype(F32) + scale_mid * (
        weighted_mid - unit_mid * jnp.mean(weighted_mid * unit_mid, axis=-1, keepdims=True)
    )
    branch = d_resid.astype(BF16)
    branch = (branch, swap(branch))
    d_attn = [dot_nt(rows, w_out).astype(BF16) for rows in branch]
    g_out = scatter_rows(
        dot_tn(
            jnp.concatenate(branch, axis=0), jnp.concatenate((attn_own, attn_oth), axis=0)
        ).astype(BF16),
        far,
    )
    dq_own, dq_oth, dk_own, dk_oth, dv_own, dv_oth, g_qgain, g_kgain = attention_backward(
        me, q_raw, k_raw, values, tables, gains, first_key,
        (attn_own, attn_oth), d_attn, totals, kv_here, group, width,
    )

    def to_input(dq_rows, dk_rows, dv_rows):
        total = dot_nt(dq_rows, w_query) + dot_nt(dk_rows, key_weight)
        return total + dot_nt(dv_rows, value_weight)

    norm_got = swap(to_input(dq_oth, dk_oth, dv_oth).astype(BF16))
    normed_all = jnp.concatenate(normed, axis=0)
    g_query = scatter_rows(
        dot_tn(normed_all, jnp.concatenate((dq_own, dq_oth), axis=0)).astype(BF16), near
    )
    dkv = jnp.concatenate(
        (
            jnp.concatenate((dk_own, dv_own), axis=1),
            jnp.concatenate((dk_oth, dv_oth), axis=1),
        ),
        axis=0,
    )
    g_kv = scatter_rows(dot_tn(normed_all, dkv).astype(BF16), far)
    d_norm = to_input(dq_own, dk_own, dv_own) + norm_got.astype(F32)
    g_attn = jnp.sum(d_norm * unit_in, axis=0)
    weighted_in = d_norm * attn_gain
    input_grad = d_resid + scale_in * (
        weighted_in - unit_in * jnp.mean(weighted_in * unit_in, axis=-1, keepdims=True)
    )
    packed = jnp.concatenate((g_attn, g_ffn, g_qgain[0], g_kgain[0]))
    packed = sum_all(packed.reshape(-1, width)).reshape(-1)
    model = attn_gain.shape[0]
    kv_columns = key_weight.shape[1]
    return (
        mixed,
        input_grad,
        packed[:model],
        g_query,
        g_kv[:, :kv_columns],
        g_kv[:, kv_columns:],
        packed[2 * model : 2 * model + width],
        packed[2 * model + width :],
        g_out.T,
        packed[model : 2 * model],
        g_gate,
        g_up,
        g_down.T,
    )


def solution(mesh):
    return jax.shard_map(
        shards,
        mesh=mesh,
        in_specs=(
            P(("dp", "tensor"), None),
            P("dp", None),
            P(),
            P(None, "tensor"),
            P(None, "tensor"),
            P(None, "tensor"),
            P(),
            P(),
            P("tensor", None),
            P(),
            P(None, "tensor"),
            P(None, "tensor"),
            P("tensor", None),
            P(("dp", "tensor"), None),
        ),
        out_specs=(
            P(("dp", "tensor"), None),
            P(("dp", "tensor"), None),
            P(),
            P("dp", "tensor"),
            P("dp", "tensor"),
            P("dp", "tensor"),
            P(),
            P(),
            P("tensor", "dp"),
            P(),
            P("dp", "tensor"),
            P("dp", "tensor"),
            P("tensor", "dp"),
        ),
        check_vma=False,
    )
```

```python
import math

import jax
import jax.numpy as jnp
from jax import lax
from jax.experimental import pallas as pl
from jax.experimental.pallas import tpu as pltpu
from jax.sharding import PartitionSpec as P

EPSILON = 1e-06
ROPE_BASE = 1000000.0
MASK_FILL = -1e30
BF16 = jnp.bfloat16
F32 = jnp.float32
VMEM_LIMIT = 56 * 1024 * 1024


def rms_scale(vectors):
    return lax.rsqrt(jnp.mean(vectors * vectors, axis=-1, keepdims=True) + EPSILON)


def dot_nn(left, right):
    return jnp.dot(left, right, preferred_element_type=F32)


def dot_tn(left, right):
    return lax.dot_general(left, right, (((0,), (0,)), ((), ())), preferred_element_type=F32)


def dot_nt(left, right):
    return lax.dot_general(left, right, (((1,), (1,)), ((), ())), preferred_element_type=F32)


def swap(array):
    return lax.ppermute(array, "tensor", [(0, 1), (1, 0)])


def layout(lengths, tokens):
    slots = jnp.arange(lengths.shape[0], dtype=jnp.int32)
    row_ends = jnp.sum(jnp.where(slots[None, :] <= slots[:, None], lengths[None, :], 0), axis=1)
    places = jnp.arange(tokens, dtype=jnp.int32)
    before = row_ends[None, :] <= places[:, None]
    label = jnp.sum(before.astype(jnp.int32), axis=1)
    starts = jnp.sum(jnp.where(before, lengths[None, :], 0), axis=1)
    first_key = jnp.where(label < lengths.shape[0], starts, tokens)
    return first_key, places - starts


def rotary(position, head_size):
    half = head_size // 2
    lane = jnp.arange(head_size, dtype=jnp.int32)
    frequency = jnp.power(ROPE_BASE, -((lane % half).astype(F32) * 2.0 / head_size))
    angles = position.astype(F32)[:, None] * frequency[None, :]
    sign = jnp.where(lane < half, -1.0, 1.0)
    return jnp.cos(angles), jnp.sin(angles) * sign[None, :]


def turn(raw, gain, cosine, sine):
    normalized = raw * rms_scale(raw) * gain
    half = raw.shape[-1] // 2
    return (normalized * cosine + pltpu.roll(normalized, half, 1) * sine).astype(BF16)


def turn_back(raw, gain, cosine, sine, grad):
    half = raw.shape[-1] // 2
    scale = rms_scale(raw)
    unit = raw * scale
    turned = grad * cosine - pltpu.roll(grad, half, 1) * sine
    gain_grad = jnp.sum(turned * unit, axis=0, keepdims=True)
    weighted = turned * gain
    back = scale * (weighted - unit * jnp.mean(weighted * unit, axis=-1, keepdims=True))
    return back.astype(BF16), gain_grad


def halves(share, me):
    own = pl.ds(pl.multiple_of(me * share, share), share)
    other = pl.ds(pl.multiple_of((1 - me) * share, share), share)
    return own, other


def forward_kernel(
    block, me_ref, q_own, q_oth, k_own, k_oth, v_own, v_oth, cos_ref, sin_ref, qg, kg, first_ref,
    o_own, o_oth, lse_ref, q_rot, k_rot, v_all, out,
):
    share = q_own.shape[0]
    tokens, width = 2 * share, q_own.shape[1]
    factor = math.log2(math.e) / math.sqrt(width)
    rows = halves(share, me_ref[0])

    @pl.when(pl.program_id(1) == 0)
    def _():
        for place, k_ref, v_ref in zip(rows, (k_own, k_oth), (v_own, v_oth)):
            k_rot[place, :] = turn(k_ref[...], kg[...], cos_ref[place, :], sin_ref[place, :])
            v_all[place, :] = v_ref[...]

    for place, q_ref in zip(rows, (q_own, q_oth)):
        q_rot[place, :] = turn(q_ref[...], qg[...], cos_ref[place, :], sin_ref[place, :])
    for start in range(0, tokens, block):
        stop = start + block
        scores = dot_nt(q_rot[start:stop, :], k_rot[:stop, :])
        key = lax.broadcasted_iota(jnp.int32, scores.shape, 1)
        row = lax.broadcasted_iota(jnp.int32, scores.shape, 0) + start
        allowed = (key >= first_ref[start:stop, :]) & (key <= row)
        terms = jnp.exp2(jnp.where(allowed, scores * factor, MASK_FILL))
        total = jnp.sum(terms, axis=-1, keepdims=True)
        total = jnp.where(total > 0.0, total, 1.0)
        result = dot_nn(terms.astype(BF16), v_all[:stop, :]) / total
        out[start:stop, :] = result.astype(BF16)
        log_total = jnp.broadcast_to(jnp.log2(total), (block, width)).T
        lse_ref[0, :, start:stop] = log_total[0:1, :]
    o_own[...] = out[rows[0], :]
    o_oth[...] = out[rows[1], :]


def backward_kernel(
    block, me_ref, q_own, q_oth, k_own, k_oth, v_own, v_oth, cos_ref, sin_ref, qg, kg, first_ref,
    o_own, o_oth, d_own, d_oth, lse_ref,
    dq_own, dq_oth, dk_own, dk_oth, dv_own, dv_oth, gq_ref, gk_ref,
    q_rot, k_rot, v_all, d_all, delta, dq_all, dk_all, dv_all,
):
    share = q_own.shape[0]
    tokens, width = 2 * share, q_own.shape[1]
    root = 1.0 / math.sqrt(width)
    factor = math.log2(math.e) * root
    rows = halves(share, me_ref[0])
    head, part = pl.program_id(0), pl.program_id(1)

    @pl.when((head == 0) & (part == 0))
    def _():
        gq_ref[...] = jnp.zeros_like(gq_ref)
        gk_ref[...] = jnp.zeros_like(gk_ref)

    @pl.when(part == 0)
    def _():
        for place, k_ref, v_ref in zip(rows, (k_own, k_oth), (v_own, v_oth)):
            k_rot[place, :] = turn(k_ref[...], kg[...], cos_ref[place, :], sin_ref[place, :])
            v_all[place, :] = v_ref[...]
        dk_all[...] = jnp.zeros_like(dk_all)
        dv_all[...] = jnp.zeros_like(dv_all)

    for place, q_ref, o_ref, d_ref in zip(
        rows, (q_own, q_oth), (o_own, o_oth), (d_own, d_oth)
    ):
        q_rot[place, :] = turn(q_ref[...], qg[...], cos_ref[place, :], sin_ref[place, :])
        d_all[place, :] = d_ref[...]
        product = o_ref[...].astype(F32) * d_ref[...].astype(F32)
        delta[:, place] = jnp.sum(product.T, axis=0, keepdims=True)
    for start in range(0, tokens, block):
        stop = start + block
        q_rows = q_rot[start:stop, :]
        d_rows = d_all[start:stop, :]
        scores = dot_nt(k_rot[:stop, :], q_rows)
        key = lax.broadcasted_iota(jnp.int32, scores.shape, 0)
        row = lax.broadcasted_iota(jnp.int32, scores.shape, 1) + start
        allowed = (key >= first_ref[:, start:stop]) & (key <= row)
        shifted = scores * factor - lse_ref[0, :, start:stop]
        probs = jnp.exp2(jnp.where(allowed, shifted, MASK_FILL))
        d_probs = dot_nt(v_all[:stop, :], d_rows)
        d_scores = (probs * (d_probs - delta[:, start:stop])).astype(BF16)
        dv_all[:stop, :] += dot_nn(probs.astype(BF16), d_rows)
        dk_all[:stop, :] += dot_nn(d_scores, q_rows)
        dq_all[start:stop, :] = dot_tn(d_scores, k_rot[:stop, :]) * root
    for place, q_ref, dq_ref in zip(rows, (q_own, q_oth), (dq_own, dq_oth)):
        back, gain_grad = turn_back(
            q_ref[...], qg[...], cos_ref[place, :], sin_ref[place, :], dq_all[place, :]
        )
        dq_ref[...] = back
        gq_ref[...] += gain_grad

    @pl.when(part == pl.num_programs(1) - 1)
    def _():
        for place, k_ref, dk_ref, dv_ref in zip(
            rows, (k_own, k_oth), (dk_own, dk_oth), (dv_own, dv_oth)
        ):
            back, gain_grad = turn_back(
                k_ref[...], kg[...], cos_ref[place, :], sin_ref[place, :], dk_all[place, :] * root
            )
            dk_ref[...] = back
            gk_ref[...] += gain_grad
            dv_ref[...] = dv_all[place, :].astype(BF16)


def attention_specs(share, width, group):
    tokens = 2 * share
    by_query = pl.BlockSpec((share, width), lambda g, j, me: (0, g * group + j))
    by_key = pl.BlockSpec((share, width), lambda g, j, me: (0, g))
    table = pl.BlockSpec((tokens, width), lambda g, j, me: (0, 0))
    gain = pl.BlockSpec((1, width), lambda g, j, me: (0, 0))
    sums = pl.BlockSpec((1, 1, tokens), lambda g, j, me: (g * group + j, 0, 0))
    return by_query, by_key, table, gain, sums


def attention_forward(me, q, k, v, tables, gains, first_key, kv_here, group, width):
    share = q[0].shape[0]
    tokens = 2 * share
    block = min(256, tokens)
    by_query, by_key, table, gain, sums = attention_specs(share, width, group)
    column = pl.BlockSpec((tokens, 1), lambda g, j, me: (0, 0))
    rows_out = jax.ShapeDtypeStruct((share, kv_here * group * width), BF16)

    def body(*refs):
        forward_kernel(block, *refs)

    return pl.pallas_call(
        body,
        grid_spec=pltpu.PrefetchScalarGridSpec(
            num_scalar_prefetch=1,
            grid=(kv_here, group),
            in_specs=[by_query] * 2 + [by_key] * 4 + [table] * 2 + [gain] * 2 + [column],
            out_specs=[by_query, by_query, sums],
            scratch_shapes=[pltpu.VMEM((tokens, width), BF16)] * 4,
        ),
        out_shape=[
            rows_out,
            rows_out,
            jax.ShapeDtypeStruct((kv_here * group, 1, tokens), F32),
        ],
        compiler_params=pltpu.CompilerParams(vmem_limit_bytes=VMEM_LIMIT),
        cost_estimate=pl.CostEstimate(
            flops=4 * kv_here * group * tokens * tokens * width,
            bytes_accessed=12 * tokens * kv_here * group * width,
            transcendentals=kv_here * group * tokens * tokens,
        ),
    )(me, *q, *k, *v, *tables, *gains, first_key[:, None])


def attention_backward(
    me, q, k, v, tables, gains, first_key, outs, d_outs, totals, kv_here, group, width
):
    share = q[0].shape[0]
    tokens = 2 * share
    block = min(256, tokens)
    by_query, by_key, table, gain, sums = attention_specs(share, width, group)
    line = pl.BlockSpec((1, tokens), lambda g, j, me: (0, 0))
    q_out = jax.ShapeDtypeStruct((share, kv_here * group * width), BF16)
    k_out = jax.ShapeDtypeStruct((share, kv_here * width), BF16)
    gain_out = jax.ShapeDtypeStruct((1, width), F32)

    def body(*refs):
        backward_kernel(block, *refs)

    return pl.pallas_call(
        body,
        grid_spec=pltpu.PrefetchScalarGridSpec(
            num_scalar_prefetch=1,
            grid=(kv_here, group),
            in_specs=[by_query] * 2
            + [by_key] * 4
            + [table] * 2
            + [gain] * 2
            + [line]
            + [by_query] * 4
            + [sums],
            out_specs=[by_query] * 2 + [by_key] * 4 + [gain] * 2,
            scratch_shapes=[pltpu.VMEM((tokens, width), BF16)] * 4
            + [pltpu.VMEM((1, tokens), F32)]
            + [pltpu.VMEM((tokens, width), F32)] * 3,
        ),
        out_shape=[q_out] * 2 + [k_out] * 4 + [gain_out] * 2,
        compiler_params=pltpu.CompilerParams(vmem_limit_bytes=VMEM_LIMIT),
        cost_estimate=pl.CostEstimate(
            flops=10 * kv_here * group * tokens * tokens * width,
            bytes_accessed=20 * tokens * kv_here * group * width,
            transcendentals=kv_here * group * tokens * tokens,
        ),
    )(me, *q, *k, *v, *tables, *gains, first_key[None, :], *outs, *d_outs, totals)


class RowSum:
    def __init__(self, partial, order):
        self.count = lax.axis_size("dp")
        self.columns = partial.shape[1]
        bits = self.count.bit_length() - 1
        self.left = list(range(bits))[::-1]
        self.order = list(order)
        self.held = partial.astype(BF16).reshape(
            (2,) * bits + (partial.shape[0] // self.count, self.columns)
        )

    def step(self):
        bit = self.order.pop(0)
        axis = self.left.index(bit)
        mine = (lax.axis_index("dp") >> bit) & 1
        kept = lax.dynamic_index_in_dim(self.held, mine, axis, keepdims=False)
        sent = lax.dynamic_index_in_dim(self.held, 1 - mine, axis, keepdims=False)
        pairs = [(i, i ^ (1 << bit)) for i in range(self.count)]
        got = lax.ppermute(sent.reshape(-1, self.columns), "dp", pairs).reshape(sent.shape)
        total = kept.astype(F32) + got.astype(F32)
        self.left.remove(bit)
        self.held = total.astype(BF16) if self.left else total

    def finish(self):
        while self.left:
            self.step()
        return self.held


def together(values, sums):
    values, held = lax.optimization_barrier((values, [s.held for s in sums]))
    for one, array in zip(sums, held):
        one.held = array
    return values


def step_all(sums):
    for one in sums:
        if one.left:
            one.step()


def sum_all(values):
    count = lax.axis_size("dp")
    values = values + swap(values)
    bit = 1
    while bit < count:
        values = values + lax.ppermute(values, "dp", [(i, i ^ bit) for i in range(count)])
        bit *= 2
    return values


def shards(
    hidden_in,
    seq_lengths,
    attn_gain,
    w_query,
    key_weight,
    value_weight,
    q_gain,
    k_gain,
    w_out,
    ffn_gain,
    w_gate,
    w_up,
    w_down,
    out_grad,
):
    width = q_gain.shape[0]
    tokens = 2 * hidden_in.shape[0]
    heads_here = w_query.shape[1] // width
    kv_here = key_weight.shape[1] // width
    group = heads_here // kv_here
    bits = lax.axis_size("dp").bit_length() - 1
    near = [0] + list(range(1, bits))
    far = [0] + list(range(2, bits)) + ([1] if bits > 1 else [])
    me = lax.axis_index("tensor").astype(jnp.int32).reshape(1)
    first_key, position = layout(seq_lengths[0], tokens)
    tables = rotary(position, width)
    gains = (q_gain[None, :], k_gain[None, :])

    resid_in = hidden_in.astype(F32)
    scale_in = rms_scale(resid_in)
    unit_in = resid_in * scale_in
    normed = (unit_in * attn_gain).astype(BF16)
    normed = (normed, swap(normed))
    grad_sent, oth_rows = lax.optimization_barrier((out_grad, normed[1]))
    normed = (normed[0], oth_rows)
    grads = (out_grad, swap(grad_sent))
    q_raw = [dot_nn(rows, w_query) for rows in normed]
    k_raw = [dot_nn(rows, key_weight) for rows in normed]
    values = [dot_nn(rows, value_weight).astype(BF16) for rows in normed]
    q_raw, grads = lax.optimization_barrier((q_raw, grads))
    attn_own, attn_oth, totals = attention_forward(
        me, q_raw, k_raw, values, tables, gains, first_key, kv_here, group, width
    )
    out_got = swap(dot_nn(attn_oth, w_out).astype(BF16))
    resid_mid = resid_in + (dot_nn(attn_own, w_out) + out_got.astype(F32))
    scale_mid = rms_scale(resid_mid)
    unit_mid = resid_mid * scale_mid
    mid = (unit_mid * ffn_gain).astype(BF16)
    mid = (mid, swap(mid))

    hidden, d_up, d_gate = [], [], []
    for rows, grad_rows in zip(mid, grads):
        gate_pre = dot_nn(rows, w_gate)
        up_pre = dot_nn(rows, w_up)
        sigmoid = jax.nn.sigmoid(gate_pre)
        activated = gate_pre * sigmoid
        hidden.append((activated * up_pre).astype(BF16))
        d_hidden = dot_nt(grad_rows, w_down)
        d_up.append((d_hidden * activated).astype(BF16))
        d_gate.append(
            (d_hidden * up_pre * sigmoid * (1.0 + gate_pre * (1.0 - sigmoid))).astype(BF16)
        )
    d_mid_got = swap((dot_nt(d_gate[1], w_gate) + dot_nt(d_up[1], w_up)).astype(BF16))
    mid_all = jnp.concatenate(mid, axis=0)
    grads_all = jnp.concatenate(grads, axis=0)
    g_gate = RowSum(dot_tn(mid_all, jnp.concatenate(d_gate, axis=0)), near)
    g_up = RowSum(dot_tn(mid_all, jnp.concatenate(d_up, axis=0)), far)
    g_down = RowSum(dot_tn(grads_all, jnp.concatenate(hidden, axis=0)), near)
    ffn_sums = [g_gate, g_up, g_down]
    step_all(ffn_sums)
    d_mid_got = together(d_mid_got, ffn_sums)
    d_mid = dot_nt(d_gate[0], w_gate) + dot_nt(d_up[0], w_up) + d_mid_got.astype(F32)
    g_ffn = jnp.sum(d_mid * unit_mid, axis=0)
    weighted_mid = d_mid * ffn_gain
    d_resid = out_grad.astype(F32) + scale_mid * (
        weighted_mid - unit_mid * jnp.mean(weighted_mid * unit_mid, axis=-1, keepdims=True)
    )
    branch = d_resid.astype(BF16)
    branch_got = swap(branch)
    step_all(ffn_sums)
    branch = (branch, together(branch_got, ffn_sums))
    d_attn = [dot_nt(rows, w_out).astype(BF16) for rows in branch]
    g_out = RowSum(
        dot_tn(jnp.concatenate(branch, axis=0), jnp.concatenate((attn_own, attn_oth), axis=0)),
        far,
    )
    down_sent = dot_nn(hidden[1], w_down).astype(BF16)
    d_attn, down_sent = together((d_attn, down_sent), [g_out])
    down_got = swap(down_sent)
    mixed = (resid_mid + (dot_nn(hidden[0], w_down) + down_got.astype(F32))).astype(BF16)
    back = attention_backward(
        me, q_raw, k_raw, values, tables, gains, first_key,
        (attn_own, attn_oth), d_attn, totals, kv_here, group, width,
    )
    sums = ffn_sums + [g_out]
    step_all(sums)
    back, mixed = together((back, mixed), sums)
    dq_own, dq_oth, dk_own, dk_oth, dv_own, dv_oth, g_qgain, g_kgain = back

    def to_input(dq_rows, dk_rows, dv_rows):
        total = dot_nt(dq_rows, w_query) + dot_nt(dk_rows, key_weight)
        return total + dot_nt(dv_rows, value_weight)

    norm_got = swap(to_input(dq_oth, dk_oth, dv_oth).astype(BF16))
    normed_all = jnp.concatenate(normed, axis=0)
    g_query = RowSum(dot_tn(normed_all, jnp.concatenate((dq_own, dq_oth), axis=0)), near)
    dkv = jnp.concatenate(
        (
            jnp.concatenate((dk_own, dv_own), axis=1),
            jnp.concatenate((dk_oth, dv_oth), axis=1),
        ),
        axis=0,
    )
    g_kv = RowSum(dot_tn(normed_all, dkv), far)
    last_sums = [g_query, g_kv]
    step_all(last_sums)
    step_all(sums)
    norm_got = together(norm_got, last_sums + sums)
    g_gate, g_up, g_down = (one.finish() for one in ffn_sums)
    g_out, g_query, g_kv = (one.finish() for one in (g_out, g_query, g_kv))
    d_norm = to_input(dq_own, dk_own, dv_own) + norm_got.astype(F32)
    g_attn = jnp.sum(d_norm * unit_in, axis=0)
    weighted_in = d_norm * attn_gain
    input_grad = d_resid + scale_in * (
        weighted_in - unit_in * jnp.mean(weighted_in * unit_in, axis=-1, keepdims=True)
    )
    packed = jnp.concatenate((g_attn, g_ffn, g_qgain[0], g_kgain[0]))
    packed = sum_all(packed.reshape(-1, width)).reshape(-1)
    model = attn_gain.shape[0]
    kv_columns = key_weight.shape[1]
    return (
        mixed,
        input_grad,
        packed[:model],
        g_query,
        g_kv[:, :kv_columns],
        g_kv[:, kv_columns:],
        packed[2 * model : 2 * model + width],
        packed[2 * model + width :],
        g_out.T,
        packed[model : 2 * model],
        g_gate,
        g_up,
        g_down.T,
    )


def solution(mesh):
    return jax.shard_map(
        shards,
        mesh=mesh,
        in_specs=(
            P(("dp", "tensor"), None),
            P("dp", None),
            P(),
            P(None, "tensor"),
            P(None, "tensor"),
            P(None, "tensor"),
            P(),
            P(),
            P("tensor", None),
            P(),
            P(None, "tensor"),
            P(None, "tensor"),
            P("tensor", None),
            P(("dp", "tensor"), None),
        ),
        out_specs=(
            P(("dp", "tensor"), None),
            P(("dp", "tensor"), None),
            P(),
            P("dp", "tensor"),
            P("dp", "tensor"),
            P("dp", "tensor"),
            P(),
            P(),
            P("tensor", "dp"),
            P(),
            P("dp", "tensor"),
            P("dp", "tensor"),
            P("tensor", "dp"),
        ),
        check_vma=False,
    )
```
